32 devices in a mesh: grp: 4 (over y, x), dev: 8 (over z, core).
Axes of the slice: x: 2, y: 2, z: 4, core: 2. Of those that a mesh axis runs over, the one named last changes fastest.
Arguments:
- memory: bfloat16 [65536, 512], P(('grp', 'dev')), may hold values from -6 to 6
- event_nodes: int32 [4096, 2], P(('grp', 'dev')), may hold values from 0 to 65535, as said below
- event_ticks: int32 [4096], P(('grp', 'dev')), may hold values from 0 to 99999
- neighbour_ids: int32 [4096, 20], P(('grp', 'dev')), may hold values from 0 to 65535, as said below
- neighbour_ticks: int32 [4096, 20], P(('grp', 'dev')), may hold values from 0 to 99999
- freq: float32 [128], replicated, may hold values from 1e-05 to 1
- phase: float32 [128], replicated, may hold values from -3.140625 to 3.140625
- w_msg1: bfloat16 [1152, 1024], replicated, may hold values from -0.1875 to 0.1875
- b_msg1: float32 [1024], replicated, may hold values from -3 to 3
- w_msg2: bfloat16 [1024, 512], replicated, may hold values from -0.1875 to 0.1875
- b_msg2: float32 [512], replicated, may hold values from -3 to 3
- w_query: bfloat16 [512, 512], replicated, may hold values from -1 to 1
- w_keyval: bfloat16 [640, 1024], replicated, may hold values from -1 to 1
- w_out: bfloat16 [512, 512], replicated, may hold values from -0.25 to 0.25
- gru_input: bfloat16 [512, 1536], replicated, may hold values from -0.25 to 0.25
- gru_hidden: bfloat16 [512, 1536], replicated, may hold values from -0.25 to 0.25
- gru_bias: float32 [2, 1536], replicated, may hold values from -3 to 3
Outputs:
- embedding: bfloat16 [4096, 512], P(('grp', 'dev'))
- new_memory: bfloat16 [65536, 512], P(('grp', 'dev'))
The draws below stay inside these ranges and needn't reach their ends.
Inputs may be any that keep to these rules, and one draw needn't show every extreme that they name: `event_nodes`: node n is held by device n // 2048 of the grp-major order; of the 256 ids of one device's events, at most 16 belong to any one owner device. `neighbour_ids`: of the 2560 neighbour ids of one device's events, at most 160 belong to any one owner device.
All inputs are finite; a program needn't handle non-finite values.
Results may differ from the reference program's by a relative error of at most 0.01.
Values may be sent and summed in bfloat16 or wider, within the bound.
A program may use at most 128 MiB of HBM per device.

```python
import math
import jax
import jax.numpy as jnp
from jax import lax

D = 512
HID = 1024
TD = 128
K = 20
HDIM = 128
EV_DEV = 128
NODE_DEV = 2048
EVENTS = 4096
NODES = 65536
CAP_E = 16
CAP_N = 160
DEVICES = 32


def owned_ids(key, salt, columns, capacity, first_row, marked):
    total = DEVICES * capacity
    count = EV_DEV * columns
    id_key = jax.random.fold_in(key, salt)
    hottest = jax.random.randint(jax.random.fold_in(id_key, 7), (), 0, DEVICES)
    owners_pool = jnp.arange(total, dtype=jnp.int32) // capacity
    specials = jax.random.randint(jax.random.fold_in(key, 303), (DEVICES,), 0, EV_DEV)
    row_index = jnp.arange(EV_DEV, dtype=jnp.int32)[:, None]
    col_index = jnp.arange(columns, dtype=jnp.int32)[None, :]

    def one_device(dkey, special):
        ranking = jax.random.permutation(jax.random.fold_in(dkey, 1), total).astype(jnp.int32)
        flagged = jnp.where(owners_pool == hottest, 0, 1).astype(jnp.int32)
        order = jnp.argsort(flagged * total + ranking)
        chosen = owners_pool[order[:count]]
        chosen = chosen[jax.random.permutation(jax.random.fold_in(dkey, 2), count)].reshape(EV_DEV, columns)
        local_rows = jax.random.randint(jax.random.fold_in(dkey, 3), (EV_DEV, columns), 0, NODE_DEV)
        hit = jnp.logical_and(row_index == special, col_index < marked)
        local_rows = jnp.where(hit, first_row + col_index, local_rows)
        return (chosen * NODE_DEV + local_rows).astype(jnp.int32)
    dkeys = jax.random.split(jax.random.fold_in(id_key, 11), DEVICES)
    return jax.vmap(one_device)(dkeys, specials).reshape(EVENTS, columns)


def draw_event_nodes(key, part):
    return owned_ids(key, 101, 2, CAP_E, 0, 1)


def draw_neighbour_ids(key, part):
    return owned_ids(key, 202, K, CAP_N, 1, 2)


def draw_memory(key, part):
    values = jax.random.truncated_normal(jax.random.fold_in(key, 41), -6.0, 6.0, (NODES, D), jnp.float32)
    return values.astype(jnp.bfloat16)


def draw_w_query(key, part):
    values = jax.random.truncated_normal(jax.random.fold_in(key, 61), -6.0, 6.0, (D, D), jnp.float32) / jnp.sqrt(jnp.float32(D))
    return values.astype(jnp.bfloat16)


def draw_w_keyval(key, part):
    values = jax.random.truncated_normal(jax.random.fold_in(key, 62), -6.0, 6.0, (D + TD, 2 * D), jnp.float32) / jnp.sqrt(jnp.float32(D + TD))
    return values.astype(jnp.bfloat16)


def touch_ends(drawn, rng, low, top_value):
    longest = drawn.shape.index(max(drawn.shape))
    spots = []
    for shift in (0, 1):
        where = [jax.random.randint(jax.random.fold_in(rng, axis), (), 0, length) for axis, length in enumerate(drawn.shape)]
        where[longest] = (where[longest] + shift) % drawn.shape[longest]
        spots.append(tuple(where))
    return drawn.at[spots[0]].set(low).at[spots[1]].set(top_value)


def normal_values(key, shape, deviation, limit, kind=jnp.bfloat16):
    return jnp.clip(deviation * jax.random.normal(key, shape, jnp.float32), -limit, limit).astype(kind)


def setup_inputs(seed: int = 0) -> dict:
    key_list = jax.random.split(jax.random.key(seed), 18)
    memory = draw_memory(jax.random.fold_in(key_list[17], 71), 0)
    event_nodes = draw_event_nodes(jax.random.fold_in(key_list[17], 71), 0)
    event_ticks = touch_ends(jax.random.randint(key_list[2], (EVENTS,), 0, 100000), jax.random.fold_in(key_list[2], 1), 0, 99999).astype(jnp.int32)
    neighbour_ids = draw_neighbour_ids(jax.random.fold_in(key_list[17], 71), 0)
    neighbour_ticks = touch_ends(jax.random.randint(key_list[4], (EVENTS, K), 0, 100000), jax.random.fold_in(key_list[4], 1), 0, 99999).astype(jnp.int32)
    freq = jnp.clip(jnp.exp(jax.random.uniform(key_list[5], (TD,), jnp.float32, math.log(9.999999747378752e-06), math.log(1.0))), 9.999999747378752e-06, 1.0)
    phase = jnp.clip(jax.random.uniform(key_list[6], (TD,), jnp.float32, -3.140625, 3.140625), -3.140625, 3.140625)
    w_msg1 = normal_values(key_list[7], (2 * D + TD, HID), (2 * D + TD) ** -0.5, 0.1875)
    b_msg1 = normal_values(key_list[8], (HID,), 0.5, 3.0, jnp.float32)
    w_msg2 = normal_values(key_list[9], (HID, D), HID ** -0.5, 0.1875)
    b_msg2 = normal_values(key_list[10], (D,), 0.5, 3.0, jnp.float32)
    w_query = draw_w_query(jax.random.fold_in(key_list[17], 71), 0)
    w_keyval = draw_w_keyval(jax.random.fold_in(key_list[17], 71), 0)
    w_out = normal_values(key_list[13], (D, D), D ** -0.5, 0.25)
    gru_input = normal_values(key_list[14], (D, 3 * D), D ** -0.5, 0.25)
    gru_hidden = normal_values(key_list[15], (D, 3 * D), D ** -0.5, 0.25)
    gru_bias = normal_values(key_list[16], (2, 3 * D), 0.5, 3.0, jnp.float32)
    return {"memory": memory, "event_nodes": event_nodes, "event_ticks": event_ticks, "neighbour_ids": neighbour_ids, "neighbour_ticks": neighbour_ticks, "freq": freq, "phase": phase, "w_msg1": w_msg1, "b_msg1": b_msg1, "w_msg2": w_msg2, "b_msg2": b_msg2, "w_query": w_query, "w_keyval": w_keyval, "w_out": w_out, "gru_input": gru_input, "gru_hidden": gru_hidden, "gru_bias": gru_bias}


def encode(ticks, freq, phase):
    return jnp.cos(ticks.astype(jnp.float32)[..., None] * freq + phase).astype(jnp.bfloat16)

def message_net(inputs, w_msg1, b_msg1, w_msg2, b_msg2):
    hidden = jnp.maximum(jnp.dot(inputs, w_msg1, preferred_element_type=jnp.float32) + b_msg1, 0.0).astype(jnp.bfloat16)
    return (jnp.dot(hidden, w_msg2, preferred_element_type=jnp.float32) + b_msg2).astype(jnp.bfloat16)

def gru_cell(mean, state, gru_input, gru_hidden, gru_bias):
    width = state.shape[1]
    gate_in = jnp.dot(mean, gru_input, preferred_element_type=jnp.float32) + gru_bias[0]
    gate_hid = jnp.dot(state, gru_hidden, preferred_element_type=jnp.float32) + gru_bias[1]
    reset = jax.nn.sigmoid(gate_in[:, :width] + gate_hid[:, :width])
    update = jax.nn.sigmoid(gate_in[:, width:2 * width] + gate_hid[:, width:2 * width])
    candidate = jnp.tanh(gate_in[:, 2 * width:] + reset * gate_hid[:, 2 * width:])
    return (1.0 - update) * candidate + update * state.astype(jnp.float32)

def attend(m_self, m_near, dt_enc, w_query, w_keyval, w_out):
    count, fanout, width = m_near.shape
    heads = width // HDIM
    query = jnp.dot(m_self, w_query, preferred_element_type=jnp.float32).astype(jnp.bfloat16).reshape(count, heads, HDIM)
    feats = jnp.concatenate([m_near, dt_enc], axis=-1).reshape(count * fanout, -1)
    keyval = jnp.dot(feats, w_keyval, preferred_element_type=jnp.float32).astype(jnp.bfloat16).reshape(count, fanout, 2, heads, HDIM)
    scores = jnp.einsum('ehc,ekhc->ehk', query.astype(jnp.float32), keyval[:, :, 0].astype(jnp.float32)) / jnp.sqrt(jnp.float32(HDIM))
    scores = scores - lax.optimization_barrier(jnp.max(scores, axis=-1, keepdims=True))
    expo = jnp.exp(scores)
    weights = (expo / lax.optimization_barrier(jnp.sum(expo, axis=-1, keepdims=True))).astype(jnp.bfloat16)
    attn = jnp.einsum('ehk,ekhc->ehc', weights.astype(jnp.float32), keyval[:, :, 1].astype(jnp.float32)).astype(jnp.bfloat16).reshape(count, width)
    return jnp.dot(attn, w_out, preferred_element_type=jnp.float32).astype(jnp.bfloat16)

def reference(memory, event_nodes, event_ticks, neighbour_ids, neighbour_ticks, freq, phase, w_msg1, b_msg1, w_msg2, b_msg2, w_query, w_keyval, w_out, gru_input, gru_hidden, gru_bias):
    nodes, width = memory.shape
    src = event_nodes[:, 0]
    dst = event_nodes[:, 1]
    m_src = memory[src]
    m_dst = memory[dst]
    enc = encode(event_ticks, freq, phase)
    msg_src = message_net(jnp.concatenate([m_src, m_dst, enc], axis=1), w_msg1, b_msg1, w_msg2, b_msg2)
    msg_dst = message_net(jnp.concatenate([m_dst, m_src, enc], axis=1), w_msg1, b_msg1, w_msg2, b_msg2)
    sums = jnp.zeros((nodes, width), jnp.float32).at[src].add(msg_src.astype(jnp.float32)).at[dst].add(msg_dst.astype(jnp.float32))
    counts = jnp.zeros((nodes,), jnp.float32).at[src].add(1.0).at[dst].add(1.0)
    mean = (sums / jnp.maximum(counts, 1.0)[:, None]).astype(jnp.bfloat16)
    blocks = nodes // NODE_DEV

    def update_block(args):
        mean_block, state_block, count_block = args
        fresh = gru_cell(mean_block, state_block, gru_input, gru_hidden, gru_bias)
        return jnp.where(count_block[:, None] > 0.0, fresh, state_block.astype(jnp.float32)).astype(jnp.bfloat16)
    new_memory = lax.map(update_block, (mean.reshape(blocks, NODE_DEV, width), memory.reshape(blocks, NODE_DEV, width), counts.reshape(blocks, NODE_DEV))).reshape(nodes, width)
    events = event_nodes.shape[0]
    eblocks = events // EV_DEV

    def embed_block(args):
        self_block, near_ids, ticks_block, near_ticks = args
        m_near = memory[near_ids]
        dt_enc = encode(ticks_block[:, None] - near_ticks, freq, phase)
        return attend(self_block, m_near, dt_enc, w_query, w_keyval, w_out)
    embedding = lax.map(embed_block, (m_src.reshape(eblocks, EV_DEV, width), neighbour_ids.reshape(eblocks, EV_DEV, -1), event_ticks.reshape(eblocks, EV_DEV), neighbour_ticks.reshape(eblocks, EV_DEV, -1))).reshape(events, width)
    return (embedding, new_memory)
```

```python
import functools

import jax
import jax.numpy as jnp
from jax import lax
from jax.experimental import pallas as pl
from jax.experimental.pallas import tpu as pltpu
from jax.sharding import PartitionSpec as P

HDIM = 128
LANE = 128
AXES = ("grp", "dev")
BF = jnp.bfloat16
F32 = jnp.float32


def encode(ticks, freq, phase):
    return jnp.cos(ticks.astype(F32)[..., None] * freq + phase).astype(BF)


def exchange(array):
    return lax.all_to_all(array, AXES, split_axis=0, concat_axis=0, tiled=True)


def contract_last(a, b):
    return lax.dot_general(a, b, (((1,), (1,)), ((), ())), preferred_element_type=F32)


def exclusive_sums(rows):
    m, n = rows.shape
    blocks = n // LANE
    flags = rows.astype(BF)
    upper = (jnp.arange(LANE)[:, None] < jnp.arange(LANE)[None, :]).astype(BF)
    inner = jnp.dot(flags.reshape(m * blocks, LANE), upper, preferred_element_type=F32)
    earlier = (jnp.arange(n)[:, None] < LANE * jnp.arange(blocks)[None, :]).astype(BF)
    before = jnp.dot(flags, earlier, preferred_element_type=F32)
    return (inner.reshape(m, blocks, LANE) + before[:, :, None]).reshape(m, n)


def slots_of(owner, owners):
    mine = owner[None, :] == jnp.arange(owners, dtype=jnp.int32)[:, None]
    return mine, jnp.sum(jnp.where(mine, exclusive_sums(mine), 0.0), axis=0).astype(jnp.int32)


def place(mine, slot, start, capacity, channels):
    owners, n = mine.shape
    left = jnp.concatenate([jnp.where(mine, c[None, :].astype(F32), 0.0).astype(BF) for c in channels])
    right = (slot[None, :] == start + jnp.arange(capacity, dtype=jnp.int32)[:, None]).astype(BF)
    out = contract_last(left, right).astype(jnp.int32)
    return [out[i * owners : (i + 1) * owners] for i in range(len(channels))]


def split_row(rows):
    return [rows // 256 + 1, rows % 256]


def join_row(parts):
    return (parts[0] - 1) * 256 + parts[1]


TICK_SHIFT = 131072


def split_info(event, delta):
    d = delta + TICK_SHIFT
    return [event + 1, d // 65536, (d // 256) % 256, d % 256]


def join_info(parts):
    event = parts[0] - 1
    delta = parts[1] * 65536 + parts[2] * 256 + parts[3] - TICK_SHIFT
    return event.reshape(-1), jnp.where(event < 0, 0, delta).reshape(-1)


def rows_at(table, rows):
    pick = (rows[:, None] == jnp.arange(table.shape[0], dtype=jnp.int32)[None, :]).astype(BF)
    return jnp.dot(pick, table, preferred_element_type=F32).astype(BF)


def attend_kernel(sizes, chunk, *refs):
    segments = len(sizes)
    xs, ds, es = refs[:segments], refs[segments : 2 * segments], refs[2 * segments : 3 * segments]
    qx_ref, qd_ref, wv_ref, wo_ref, out_ref, scores = refs[3 * segments :]
    rows = qx_ref.shape[0]
    events, width = out_ref.shape
    heads = rows // events
    scale = 1.0 / (HDIM**0.5)
    event = lax.broadcasted_iota(jnp.int32, (rows, 1), 0) % events
    top = jnp.full((rows, 1), -3.0e38, F32)
    steps = []
    base = 0
    for i, size in enumerate(sizes):
        for at in range(0, size, chunk):
            steps.append((i, at, min(chunk, size - at), base + at))
        base += size
    for i, at, length, column in steps:
        x = xs[i][at : at + length, :]
        d = ds[i][at : at + length, :]
        s = (contract_last(qx_ref[...], x) + contract_last(qd_ref[...], d)) * scale
        s = jnp.where(es[i][:, at : at + length] == event, s, -3.0e38)
        scores[:, column : column + length] = s
        top = jnp.maximum(top, jnp.max(s, axis=1, keepdims=True))
    total = jnp.zeros((rows, 1), F32)
    ctx_x = jnp.zeros((rows, width), F32)
    ctx_d = jnp.zeros((rows, qd_ref.shape[1]), F32)
    for i, at, length, column in steps:
        p = jnp.exp(scores[:, column : column + length] - top)
        total = total + jnp.sum(p, axis=1, keepdims=True)
        w = p.astype(BF)
        ctx_x = ctx_x + jnp.dot(w, xs[i][at : at + length, :], preferred_element_type=F32)
        ctx_d = ctx_d + jnp.dot(w, ds[i][at : at + length, :], preferred_element_type=F32)
    inverse = 1.0 / total
    ctx_x = (ctx_x * inverse).astype(BF)
    ctx_d = (ctx_d * inverse).astype(BF)
    parts = []
    for h in range(heads):
        r = slice(h * events, (h + 1) * events)
        c = slice(width + h * HDIM, width + (h + 1) * HDIM)
        part = jnp.dot(ctx_x[r], wv_ref[:width, c], preferred_element_type=F32)
        part = part + jnp.dot(ctx_d[r], wv_ref[width:, c], preferred_element_type=F32)
        parts.append(part.astype(BF))
    attn = jnp.concatenate(parts, axis=1)
    out_ref[...] = jnp.dot(attn, wo_ref[...], preferred_element_type=F32).astype(BF)


def attend(segments, qx, qd, w_keyval, w_out, events, width):
    sizes = tuple(x.shape[0] for x, _, _ in segments)
    rows, total = qx.shape[0], sum(sizes)
    features = width + qd.shape[1]
    args = (
        [x for x, _, _ in segments]
        + [d for _, d, _ in segments]
        + [e.reshape(1, -1) for _, _, e in segments]
        + [qx, qd, w_keyval, w_out]
    )
    return pl.pallas_call(
        functools.partial(attend_kernel, sizes, 512),
        out_shape=jax.ShapeDtypeStruct((events, width), BF),
        in_specs=[pl.BlockSpec(memory_space=pltpu.VMEM)] * len(args),
        out_specs=pl.BlockSpec(memory_space=pltpu.VMEM),
        scratch_shapes=[pltpu.VMEM((rows, total), F32)],
        compiler_params=pltpu.CompilerParams(vmem_limit_bytes=44 * 1024 * 1024),
        cost_estimate=pl.CostEstimate(
            flops=4 * rows * total * features,
            bytes_accessed=2 * total * features + 4 * 1024 * 1024,
            transcendentals=rows * total,
        ),
    )(*args)


def on_device(
    memory,
    event_nodes,
    event_ticks,
    neighbour_ids,
    neighbour_ticks,
    freq,
    phase,
    w_msg1,
    b_msg1,
    w_msg2,
    b_msg2,
    w_query,
    w_keyval,
    w_out,
    gru_input,
    gru_hidden,
    gru_bias,
):
    owners = lax.axis_size(AXES)
    me = lax.axis_index(AXES)
    node_dev, width = memory.shape
    events = event_nodes.shape[0]
    fanout = neighbour_ids.shape[1]
    cap_e = 4 * events // owners
    cap_n = 2 * fanout * events // owners
    base_n = 3 * cap_n // 5
    spill_n = fanout * events // owners
    spill_pad = -(-spill_n // LANE) * LANE

    ends = event_nodes.T.reshape(-1)
    end_mine, end_slot = slots_of(ends // node_dev, owners)
    end_req = join_row(place(end_mine, end_slot, 0, cap_e, split_row(ends % node_dev)))
    near = neighbour_ids.reshape(-1)
    near_mine, near_slot = slots_of(near // node_dev, owners)
    near_rows = split_row(near % node_dev)
    near_req = join_row(place(near_mine, near_slot, 0, base_n, near_rows))
    spilled = near_slot >= base_n
    spill_rank = exclusive_sums(spilled[None, :])[0].astype(jnp.int32)
    spill_mine = spilled[None, :]
    hi, mid, low = place(
        spill_mine, spill_rank, 0, spill_n, [near // 65536, (near // 256) % 256, near % 256]
    )
    (used,) = place(spill_mine, spill_rank, 0, spill_n, [jnp.ones_like(near)])
    spill_ids = jnp.where(used > 0, hi * 65536 + mid * 256 + low, -1)
    spill_count = jnp.sum(spilled.astype(jnp.int32)).reshape(1, 1)
    sent = jnp.concatenate(
        [
            end_req,
            near_req,
            jnp.broadcast_to(spill_ids, (owners, spill_n)),
            jnp.broadcast_to(spill_count, (owners, 1)),
        ],
        axis=1,
    )
    got = exchange(sent)
    end_got = got[:, :cap_e].reshape(-1)
    near_got = got[:, cap_e : cap_e + base_n].reshape(-1)
    spill_got = got[:, cap_e + base_n : cap_e + base_n + spill_n].reshape(-1)
    overfull = jnp.max(got[:, -1]) > spill_n

    states = rows_at(memory, end_got)
    end_rows = exchange(states.reshape(owners, cap_e, width)).reshape(-1, width)
    near_x = exchange(rows_at(memory, near_got).reshape(owners, base_n, width)).reshape(-1, width)
    spill_local = jnp.where(spill_got // node_dev == me, spill_got % node_dev, -1)
    spill_local = jnp.where(spill_got >= 0, spill_local, -1)
    spill_x = lax.psum_scatter(rows_at(memory, spill_local), AXES, scatter_dimension=0, tiled=True)
    spill_x = jnp.pad(spill_x, ((0, spill_pad - spill_n), (0, 0)))

    end_pos = (ends // node_dev) * cap_e + end_slot
    both = rows_at(end_rows, end_pos)
    m_src, m_dst = both[:events], both[events:]
    enc = encode(event_ticks, freq, phase)
    inputs = jnp.concatenate(
        [jnp.concatenate([m_src, m_dst, enc], axis=1), jnp.concatenate([m_dst, m_src, enc], axis=1)]
    )
    hidden = jnp.maximum(jnp.dot(inputs, w_msg1, preferred_element_type=F32) + b_msg1, 0.0).astype(BF)
    messages = (jnp.dot(hidden, w_msg2, preferred_element_type=F32) + b_msg2).astype(BF)
    slots = jnp.arange(owners * cap_e, dtype=jnp.int32)
    outgoing = jnp.dot(
        (slots[:, None] == end_pos[None, :]).astype(BF), messages, preferred_element_type=F32
    ).astype(BF)
    arrived = exchange(outgoing.reshape(owners, cap_e, width)).reshape(-1, width)

    valid = end_got >= 0
    same = jnp.logical_and(end_got[:, None] == end_got[None, :], valid[:, None])
    sums = jnp.dot(same.astype(BF), arrived, preferred_element_type=F32)
    counts = jnp.sum(same.astype(F32), axis=1)
    mean = (sums / jnp.maximum(counts, 1.0)[:, None]).astype(BF)
    gate_in = jnp.dot(mean, gru_input, preferred_element_type=F32) + gru_bias[0]
    gate_hid = jnp.dot(states, gru_hidden, preferred_element_type=F32) + gru_bias[1]
    reset = jax.nn.sigmoid(gate_in[:, :width] + gate_hid[:, :width])
    update = jax.nn.sigmoid(gate_in[:, width : 2 * width] + gate_hid[:, width : 2 * width])
    candidate = jnp.tanh(gate_in[:, 2 * width :] + reset * gate_hid[:, 2 * width :])
    fresh = ((1.0 - update) * candidate + update * states.astype(F32)).astype(BF)
    repeats = jnp.sum(jnp.logical_and(same, slots[None, :] < slots[:, None]).astype(F32), axis=1)
    first = jnp.where(jnp.logical_and(valid, repeats == 0.0), end_got, -1)
    chosen = jnp.arange(node_dev, dtype=jnp.int32)[:, None] == first[None, :]
    placed = jnp.dot(chosen.astype(BF), fresh, preferred_element_type=F32)
    touched = jnp.sum(chosen.astype(F32), axis=1) > 0.0
    new_memory = jnp.where(touched[:, None], placed.astype(BF), memory)

    heads = width // HDIM
    query = jnp.dot(m_src, w_query, preferred_element_type=F32).astype(BF)
    keys = w_keyval[:, :width].reshape(-1, heads, HDIM)
    lifted = jnp.einsum(
        "ehc,dhc->hed", query.reshape(events, heads, HDIM), keys, preferred_element_type=F32
    ).astype(BF)
    qx = lifted[:, :, :width].reshape(heads * events, width)
    qd = lifted[:, :, width:].reshape(heads * events, -1)
    near_event = jnp.repeat(jnp.arange(events, dtype=jnp.int32), fanout)
    delta = (event_ticks[:, None] - neighbour_ticks).reshape(-1)
    info = split_info(near_event, delta)

    def segment(x, parts, pad=0):
        event, ticks = join_info(parts)
        event = jnp.pad(event, (0, pad), constant_values=-1)
        ticks = jnp.pad(ticks, (0, pad))
        return (x, encode(ticks, freq, phase), event)

    base = segment(near_x, place(near_mine, near_slot, 0, base_n, info))

    spill = segment(spill_x, place(spill_mine, spill_rank, 0, spill_n, info), spill_pad - spill_n)

    def usual():
        return attend([base, spill], qx, qd, w_keyval, w_out, events, width)

    def crowded():
        rest_n = cap_n - base_n
        request = join_row(place(near_mine, near_slot, base_n, rest_n, near_rows))
        rows = rows_at(memory, exchange(request).reshape(-1))
        x = exchange(rows.reshape(owners, rest_n, width)).reshape(-1, width)
        rest = segment(x, place(near_mine, near_slot, base_n, rest_n, info))
        return attend([base, rest], qx, qd, w_keyval, w_out, events, width)

    embedding = lax.cond(overfull, crowded, usual)
    return (embedding, new_memory)


def solution(mesh):
    rows, flat = P(AXES, None), P(AXES)
    in_specs = (rows, rows, flat, rows, rows) + (P(),) * 12
    return jax.shard_map(
        on_device, mesh=mesh, in_specs=in_specs, out_specs=(rows, rows), check_vma=False
    )
```

```python
import functools

import jax
import jax.numpy as jnp
from jax import lax
from jax.experimental import pallas as pl
from jax.experimental.pallas import tpu as pltpu
from jax.sharding import PartitionSpec as P

HDIM = 128
LANE = 128
AXES = ("grp", "dev")
BF = jnp.bfloat16
F32 = jnp.float32


def encode(ticks, freq, phase):
    return jnp.cos(ticks.astype(F32)[..., None] * freq + phase).astype(BF)


def exchange(array):
    return lax.all_to_all(array, AXES, split_axis=0, concat_axis=0, tiled=True)


def contract_last(a, b):
    return lax.dot_general(a, b, (((1,), (1,)), ((), ())), preferred_element_type=F32)


def exclusive_sums(rows):
    m, n = rows.shape
    blocks = n // LANE
    flags = rows.astype(BF)
    upper = (jnp.arange(LANE)[:, None] < jnp.arange(LANE)[None, :]).astype(BF)
    inner = jnp.dot(flags.reshape(m * blocks, LANE), upper, preferred_element_type=F32)
    earlier = (jnp.arange(n)[:, None] < LANE * jnp.arange(blocks)[None, :]).astype(BF)
    before = jnp.dot(flags, earlier, preferred_element_type=F32)
    return (inner.reshape(m, blocks, LANE) + before[:, :, None]).reshape(m, n)


def slots_of(owner, owners):
    mine = owner[None, :] == jnp.arange(owners, dtype=jnp.int32)[:, None]
    return mine, jnp.sum(jnp.where(mine, exclusive_sums(mine), 0.0), axis=0).astype(jnp.int32)


def place(mine, slot, start, capacity, channels):
    owners, n = mine.shape
    left = jnp.concatenate([jnp.where(mine, c[None, :].astype(F32), 0.0).astype(BF) for c in channels])
    right = (slot[None, :] == start + jnp.arange(capacity, dtype=jnp.int32)[:, None]).astype(BF)
    out = contract_last(left, right).astype(jnp.int32)
    return [out[i * owners : (i + 1) * owners] for i in range(len(channels))]


def split_row(rows):
    return [rows // 256 + 1, rows % 256]


def join_row(parts):
    return (parts[0] - 1) * 256 + parts[1]


TICK_SHIFT = 131072


def split_info(event, delta):
    d = delta + TICK_SHIFT
    return [event + 1, d // 65536, (d // 256) % 256, d % 256]


def join_info(parts):
    event = parts[0] - 1
    delta = parts[1] * 65536 + parts[2] * 256 + parts[3] - TICK_SHIFT
    return event.reshape(-1), jnp.where(event < 0, 0, delta).reshape(-1)


def rows_at(table, rows):
    pick = (rows[:, None] == jnp.arange(table.shape[0], dtype=jnp.int32)[None, :]).astype(BF)
    return jnp.dot(pick, table, preferred_element_type=F32).astype(BF)


def halving_sum(blocks, owners, me):
    width = owners.bit_length() - 1
    shape = blocks.shape[1:]
    left = list(range(width - 1, -1, -1))
    acc = blocks.reshape((2,) * width + shape)
    for bit in [0] + list(range(3, width)) + [1, 2]:
        axis = left.index(bit)
        left.pop(axis)
        low = lax.index_in_dim(acc, 0, axis, keepdims=False)
        high = lax.index_in_dim(acc, 1, axis, keepdims=False)
        upper = (me >> bit) % 2 == 1
        pairs = [(i, i ^ (1 << bit)) for i in range(owners)]
        came = lax.ppermute(jnp.where(upper, low, high), AXES, pairs)
        acc = jnp.where(upper, high, low) + came
    return acc


def attend_kernel(sizes, chunk, *refs):
    segments = len(sizes)
    xs, ds, es = refs[:segments], refs[segments : 2 * segments], refs[2 * segments : 3 * segments]
    qx_ref, qd_ref, wv_ref, wo_ref, out_ref, scores = refs[3 * segments :]
    rows = qx_ref.shape[0]
    events, width = out_ref.shape
    heads = rows // events
    scale = 1.0 / (HDIM**0.5)
    event = lax.broadcasted_iota(jnp.int32, (rows, 1), 0) % events
    top = jnp.full((rows, 1), -3.0e38, F32)
    steps = []
    base = 0
    for i, size in enumerate(sizes):
        for at in range(0, size, chunk):
            steps.append((i, at, min(chunk, size - at), base + at))
        base += size
    for i, at, length, column in steps:
        x = xs[i][at : at + length, :]
        d = ds[i][at : at + length, :]
        s = (contract_last(qx_ref[...], x) + contract_last(qd_ref[...], d)) * scale
        s = jnp.where(es[i][:, at : at + length] == event, s, -3.0e38)
        scores[:, column : column + length] = s
        top = jnp.maximum(top, jnp.max(s, axis=1, keepdims=True))
    total = jnp.zeros((rows, 1), F32)
    ctx_x = jnp.zeros((rows, width), F32)
    ctx_d = jnp.zeros((rows, qd_ref.shape[1]), F32)
    for i, at, length, column in steps:
        p = jnp.exp(scores[:, column : column + length] - top)
        total = total + jnp.sum(p, axis=1, keepdims=True)
        w = p.astype(BF)
        ctx_x = ctx_x + jnp.dot(w, xs[i][at : at + length, :], preferred_element_type=F32)
        ctx_d = ctx_d + jnp.dot(w, ds[i][at : at + length, :], preferred_element_type=F32)
    inverse = 1.0 / total
    ctx_x = (ctx_x * inverse).astype(BF)
    ctx_d = (ctx_d * inverse).astype(BF)
    parts = []
    for h in range(heads):
        r = slice(h * events, (h + 1) * events)
        c = slice(width + h * HDIM, width + (h + 1) * HDIM)
        part = jnp.dot(ctx_x[r], wv_ref[:width, c], preferred_element_type=F32)
        part = part + jnp.dot(ctx_d[r], wv_ref[width:, c], preferred_element_type=F32)
        parts.append(part.astype(BF))
    attn = jnp.concatenate(parts, axis=1)
    out_ref[...] = jnp.dot(attn, wo_ref[...], preferred_element_type=F32).astype(BF)


def attend(segments, qx, qd, w_keyval, w_out, events, width):
    sizes = tuple(x.shape[0] for x, _, _ in segments)
    rows, total = qx.shape[0], sum(sizes)
    features = width + qd.shape[1]
    args = (
        [x for x, _, _ in segments]
        + [d for _, d, _ in segments]
        + [e.reshape(1, -1) for _, _, e in segments]
        + [qx, qd, w_keyval, w_out]
    )
    return pl.pallas_call(
        functools.partial(attend_kernel, sizes, 512),
        out_shape=jax.ShapeDtypeStruct((events, width), BF),
        in_specs=[pl.BlockSpec(memory_space=pltpu.VMEM)] * len(args),
        out_specs=pl.BlockSpec(memory_space=pltpu.VMEM),
        scratch_shapes=[pltpu.VMEM((rows, total), F32)],
        compiler_params=pltpu.CompilerParams(vmem_limit_bytes=44 * 1024 * 1024),
        cost_estimate=pl.CostEstimate(
            flops=4 * rows * total * features,
            bytes_accessed=2 * total * features + 4 * 1024 * 1024,
            transcendentals=rows * total,
        ),
    )(*args)


def on_device(
    memory,
    event_nodes,
    event_ticks,
    neighbour_ids,
    neighbour_ticks,
    freq,
    phase,
    w_msg1,
    b_msg1,
    w_msg2,
    b_msg2,
    w_query,
    w_keyval,
    w_out,
    gru_input,
    gru_hidden,
    gru_bias,
):
    owners = lax.axis_size(AXES)
    me = lax.axis_index(AXES)
    node_dev, width = memory.shape
    events = event_nodes.shape[0]
    fanout = neighbour_ids.shape[1]
    cap_e = 4 * events // owners
    cap_n = 2 * fanout * events // owners
    base_n = 3 * cap_n // 5
    spill_n = fanout * events // owners
    spill_pad = -(-spill_n // LANE) * LANE

    ends = event_nodes.T.reshape(-1)
    end_mine, end_slot = slots_of(ends // node_dev, owners)
    end_req = join_row(place(end_mine, end_slot, 0, cap_e, split_row(ends % node_dev)))
    near = neighbour_ids.reshape(-1)
    near_mine, near_slot = slots_of(near // node_dev, owners)
    near_rows = split_row(near % node_dev)
    near_req = join_row(place(near_mine, near_slot, 0, base_n, near_rows))
    spilled = near_slot >= base_n
    spill_rank = exclusive_sums(spilled[None, :])[0].astype(jnp.int32)
    spill_mine = spilled[None, :]
    hi, mid, low = place(
        spill_mine, spill_rank, 0, spill_n, [near // 65536, (near // 256) % 256, near % 256]
    )
    (used,) = place(spill_mine, spill_rank, 0, spill_n, [jnp.ones_like(near)])
    spill_ids = jnp.where(used > 0, hi * 65536 + mid * 256 + low, -1)
    spill_count = jnp.sum(spilled.astype(jnp.int32)).reshape(1, 1)
    sent = jnp.concatenate(
        [
            end_req,
            near_req,
            jnp.broadcast_to(spill_ids, (owners, spill_n)),
            jnp.broadcast_to(spill_count, (owners, 1)),
        ],
        axis=1,
    )
    got = exchange(sent)
    end_got = got[:, :cap_e].reshape(-1)
    near_got = got[:, cap_e : cap_e + base_n].reshape(-1)
    spill_got = got[:, cap_e + base_n : cap_e + base_n + spill_n].reshape(-1)
    overfull = jnp.max(got[:, -1]) > spill_n

    states = rows_at(memory, end_got)
    end_rows = exchange(states.reshape(owners, cap_e, width)).reshape(-1, width)
    near_x = exchange(rows_at(memory, near_got).reshape(owners, base_n, width)).reshape(-1, width)

    end_pos = (ends // node_dev) * cap_e + end_slot
    both = rows_at(end_rows, end_pos)
    m_src, m_dst = both[:events], both[events:]
    enc = encode(event_ticks, freq, phase)
    inputs = jnp.concatenate(
        [jnp.concatenate([m_src, m_dst, enc], axis=1), jnp.concatenate([m_dst, m_src, enc], axis=1)]
    )
    hidden = jnp.maximum(jnp.dot(inputs, w_msg1, preferred_element_type=F32) + b_msg1, 0.0).astype(BF)
    messages = (jnp.dot(hidden, w_msg2, preferred_element_type=F32) + b_msg2).astype(BF)
    slots = jnp.arange(owners * cap_e, dtype=jnp.int32)
    outgoing = jnp.dot(
        (slots[:, None] == end_pos[None, :]).astype(BF), messages, preferred_element_type=F32
    ).astype(BF)
    arrived = exchange(outgoing.reshape(owners, cap_e, width)).reshape(-1, width)

    spill_local = jnp.where(spill_got // node_dev == me, spill_got % node_dev, -1)
    spill_local = jnp.where(spill_got >= 0, spill_local, -1)
    spill_local, arrived = lax.optimization_barrier((spill_local, arrived))
    spill_x = halving_sum(rows_at(memory, spill_local).reshape(owners, spill_n, width), owners, me)
    spill_x = jnp.pad(spill_x, ((0, spill_pad - spill_n), (0, 0)))

    valid = end_got >= 0
    same = jnp.logical_and(end_got[:, None] == end_got[None, :], valid[:, None])
    sums = jnp.dot(same.astype(BF), arrived, preferred_element_type=F32)
    counts = jnp.sum(same.astype(F32), axis=1)
    mean = (sums / jnp.maximum(counts, 1.0)[:, None]).astype(BF)
    gate_in = jnp.dot(mean, gru_input, preferred_element_type=F32) + gru_bias[0]
    gate_hid = jnp.dot(states, gru_hidden, preferred_element_type=F32) + gru_bias[1]
    reset = jax.nn.sigmoid(gate_in[:, :width] + gate_hid[:, :width])
    update = jax.nn.sigmoid(gate_in[:, width : 2 * width] + gate_hid[:, width : 2 * width])
    candidate = jnp.tanh(gate_in[:, 2 * width :] + reset * gate_hid[:, 2 * width :])
    fresh = ((1.0 - update) * candidate + update * states.astype(F32)).astype(BF)
    repeats = jnp.sum(jnp.logical_and(same, slots[None, :] < slots[:, None]).astype(F32), axis=1)
    first = jnp.where(jnp.logical_and(valid, repeats == 0.0), end_got, -1)
    chosen = jnp.arange(node_dev, dtype=jnp.int32)[:, None] == first[None, :]
    placed = jnp.dot(chosen.astype(BF), fresh, preferred_element_type=F32)
    touched = jnp.sum(chosen.astype(F32), axis=1) > 0.0
    new_memory = jnp.where(touched[:, None], placed.astype(BF), memory)

    heads = width // HDIM
    query = jnp.dot(m_src, w_query, preferred_element_type=F32).astype(BF)
    keys = w_keyval[:, :width].reshape(-1, heads, HDIM)
    lifted = jnp.einsum(
        "ehc,dhc->hed", query.reshape(events, heads, HDIM), keys, preferred_element_type=F32
    ).astype(BF)
    qx = lifted[:, :, :width].reshape(heads * events, width)
    qd = lifted[:, :, width:].reshape(heads * events, -1)
    near_event = jnp.repeat(jnp.arange(events, dtype=jnp.int32), fanout)
    delta = (event_ticks[:, None] - neighbour_ticks).reshape(-1)
    info = split_info(near_event, delta)

    def segment(x, parts, pad=0):
        event, ticks = join_info(parts)
        event = jnp.pad(event, (0, pad), constant_values=-1)
        ticks = jnp.pad(ticks, (0, pad))
        return (x, encode(ticks, freq, phase), event)

    base = segment(near_x, place(near_mine, near_slot, 0, base_n, info))

    spill = segment(spill_x, place(spill_mine, spill_rank, 0, spill_n, info), spill_pad - spill_n)

    def usual():
        return attend([base, spill], qx, qd, w_keyval, w_out, events, width)

    def crowded():
        rest_n = cap_n - base_n
        request = join_row(place(near_mine, near_slot, base_n, rest_n, near_rows))
        rows = rows_at(memory, exchange(request).reshape(-1))
        x = exchange(rows.reshape(owners, rest_n, width)).reshape(-1, width)
        rest = segment(x, place(near_mine, near_slot, base_n, rest_n, info))
        return attend([base, rest], qx, qd, w_keyval, w_out, events, width)

    embedding = lax.cond(overfull, crowded, usual)
    return (embedding, new_memory)


def solution(mesh):
    rows, flat = P(AXES, None), P(AXES)
    in_specs = (rows, rows, flat, rows, rows) + (P(),) * 12
    return jax.shard_map(
        on_device, mesh=mesh, in_specs=in_specs, out_specs=(rows, rows), check_vma=False
    )
```
